512 devices in a mesh: ctx: 32 (over y_lo, z), head: 8 (over x, core), grp: 2 (over y_hi).
Axes of the slice: x: 4, y: 4 (y_hi: 2, y_lo: 2; y = y_hi * 2 + y_lo), z: 16, core: 2. Of those that a mesh axis runs over, the one named last changes fastest.
Arguments:
- tokens: bfloat16 [2, 8192, 3072], P('grp', 'ctx', 'head'), may hold values from -6 to 6
- modulation: bfloat16 [2, 3, 3072], P('grp'), may hold values from -3 to 3
- w_qkv: bfloat16 [3072, 3, 2048], P(('ctx', 'grp'), None, 'head'), may hold values from -0.09021098 to 0.09021098
- query_gain: float32 [128], replicated, may hold values from 1 to 6
- key_gain: float32 [128], replicated, may hold values from 1 to 6
- w_out: bfloat16 [2048, 3072], P('head'), may hold values from -0.125 to 0.125
Outputs:
- branch: bfloat16 [2, 8192, 3072], P('grp', 'ctx', 'head')
The draws below stay inside these ranges and needn't reach their ends.
All inputs are finite; a program needn't handle non-finite values.
Results may differ from the reference program's by a relative error of at most 0.02.
The reference program's roundings to bfloat16 on the way count: a program that leaves them out, or rounds other values in their place, can miss the bound.
Values may be sent and summed in bfloat16 or wider, within the bound.
A program may use at most 64 MiB of HBM per device.

```python
import math
import jax
import jax.numpy as jnp
from jax import lax

D = 3072
HDIM = 128
HD = 2
HEADS = 16
SEQ = 8192
N_HEAD = 8
N_GRP = 2


def clipped_normal(key, shape, limit):
    return jnp.clip(jax.random.normal(key, shape, jnp.float32), -limit, limit)


def draw_tokens(key, part):
    key = jax.random.fold_in(key, 11)
    base_key = jax.random.fold_in(key, 0)
    states = clipped_normal(base_key, (N_GRP, SEQ, D), 6.0)
    return states.astype(jnp.bfloat16)


def draw_w_qkv(key, part):
    key = jax.random.fold_in(key, 23)
    weight_key = jax.random.fold_in(key, 0)
    weights = clipped_normal(weight_key, (D, 3, HEADS * HDIM), 4.95) * D ** (-0.5)
    return weights.astype(jnp.bfloat16)


def draw_query_gain(key, part):
    key = jax.random.fold_in(key, 37)
    return jnp.exp(jax.random.uniform(key, (HDIM,), jnp.float32, 0.0, math.log(3.0)))


def draw_key_gain(key, part):
    key = jax.random.fold_in(key, 41)
    return jnp.exp(jax.random.uniform(key, (HDIM,), jnp.float32, 0.0, math.log(3.0)))


def block_scale(own_key, extent, shards, least, high):
    level = 1.0
    for dim, blocks in shards:
        draws = jax.random.uniform(jax.random.fold_in(jax.random.fold_in(own_key, 6), dim), (blocks,), jnp.float32, least / len(shards), high / len(shards))
        level = level * jnp.repeat(jnp.exp(draws), extent[dim] // blocks).reshape((-1,) + (1,) * (len(extent) - 1 - dim))
    return level


def centred(own_key, extent, scale, bound, cuts=(), dtype=jnp.bfloat16):
    entries = jax.random.normal(own_key, extent, jnp.float32) * scale
    if len(cuts) > 0:
        entries = block_scale(own_key, extent, cuts, -0.22, 0.18) * entries
    return jnp.clip(entries, min=-bound, max=bound).astype(dtype)


def setup_inputs(seed: int = 0) -> dict:
    streams_of = jax.random.split(jax.random.key(seed), 7)
    tokens = draw_tokens(jax.random.fold_in(streams_of[6], 71), 0)
    modulation = centred(streams_of[1], (N_GRP, 3, D), 0.5, 3.0, ((0, 2),))
    w_qkv = draw_w_qkv(jax.random.fold_in(streams_of[6], 71), 0)
    query_gain = draw_query_gain(jax.random.fold_in(streams_of[6], 71), 0)
    key_gain = draw_key_gain(jax.random.fold_in(streams_of[6], 71), 0)
    w_out = centred(streams_of[5], (HEADS * HDIM, D), (HEADS * HDIM) ** -0.5, 0.125, ((0, 8),))
    return {"tokens": tokens, "modulation": modulation, "w_qkv": w_qkv, "query_gain": query_gain, "key_gain": key_gain, "w_out": w_out}


def norm_heads(values, gain):
    mean_square = lax.optimization_barrier(jnp.mean(values * values, axis=-1, keepdims=True))
    return (values * lax.rsqrt(mean_square + 1e-06) * gain).astype(jnp.bfloat16)

def one_sequence(hidden, modulation, w_qkv, query_gain, key_gain, w_out):
    floats = hidden.astype(jnp.float32)
    center = lax.optimization_barrier(jnp.mean(floats, axis=-1, keepdims=True))
    spread = lax.optimization_barrier(jnp.mean((floats - center) ** 2, axis=-1, keepdims=True))
    normed = (floats - center) * lax.rsqrt(spread + 1e-06)
    mods = modulation.astype(jnp.float32)
    modulated = (normed * (1.0 + mods[1]) + mods[0]).astype(jnp.bfloat16)
    qkv = jnp.dot(modulated, w_qkv.reshape(D, 3 * HEADS * HDIM), preferred_element_type=jnp.float32)
    qkv = qkv.reshape(SEQ, 3, HEADS, HDIM)
    queries = norm_heads(qkv[:, 0], query_gain).transpose(1, 0, 2)
    keys = norm_heads(qkv[:, 1], key_gain).transpose(1, 0, 2)
    values = qkv[:, 2].astype(jnp.bfloat16).transpose(1, 0, 2)

    def head_attention(triple):
        head_q, head_k, head_v = triple
        scores = jnp.dot(head_q, head_k.T, preferred_element_type=jnp.float32) * HDIM ** (-0.5)
        highest = lax.optimization_barrier(jnp.max(scores, axis=-1, keepdims=True))
        weights = jnp.exp(scores - highest)
        totals = lax.optimization_barrier(jnp.sum(weights, axis=-1, keepdims=True))
        mixed = jnp.dot(weights.astype(jnp.bfloat16), head_v, preferred_element_type=jnp.float32)
        return mixed / totals
    attended = lax.map(head_attention, (queries, keys, values))
    attended = attended.transpose(1, 0, 2).reshape(SEQ, HEADS * HDIM).astype(jnp.bfloat16)
    width = HD * HDIM
    projected = jnp.zeros((SEQ, D), jnp.float32)
    for group in range(N_HEAD):
        partial_sum = jnp.dot(attended[:, group * width:(group + 1) * width], w_out[group * width:(group + 1) * width], preferred_element_type=jnp.float32)
        projected = projected + partial_sum.astype(jnp.bfloat16).astype(jnp.float32)
    return (mods[2] * projected).astype(jnp.bfloat16)

def reference(tokens, modulation, w_qkv, query_gain, key_gain, w_out):
    return jnp.stack([one_sequence(tokens[index], modulation[index], w_qkv, query_gain, key_gain, w_out) for index in range(N_GRP)])
```

```python
import functools

import jax
import jax.numpy as jnp
import numpy as np
from jax import lax
from jax.experimental import pallas as pl
from jax.experimental.pallas import tpu as pltpu
from jax.sharding import PartitionSpec as P

MESH = pl.DeviceIdType.MESH
BF16 = jnp.bfloat16
F32 = jnp.float32
NZ, NH, HDIM = 16, 8, 128
TOK, FEAT, WIDTH = 256, 384, 3072
PART = 32
QKV = 3 * HDIM
BATCHES, SLOTS = 4, 4
ROWS = SLOTS * PART
N_SEMS = 160
EXP2_SCALE = float(HDIM ** (-0.5) * np.log2(np.e))


def head_of(z):
    return lax.rem(z, 4) * 4 + z // 4


def holder_shift(z):
    return 1 - jnp.minimum(lax.rem(z, 15), 1)


def kernel(
    tok,
    mod,
    w_in,
    q_gain,
    k_gain,
    w_out,
    out,
    wp,
    ta,
    xb,
    wb,
    qb,
    kv,
    wo,
    os,
    ob,
    m_s,
    l_s,
    a_s,
    send_sem,
    recv_sem,
):
    c = lax.axis_index("ctx")
    h = lax.axis_index("head")
    yhi = lax.axis_index("grp")
    ylo, z = c // NZ, lax.rem(c, NZ)
    y = 2 * yhi + ylo

    def dev(y, z, h):
        return (lax.rem(y, 2) * NZ + z, h, y // 2)

    def at_z(k):
        return dev(y, lax.rem(z + k + NZ, NZ), h)

    def at_y(k):
        return dev(lax.rem(y + k + 4, 4), z, h)

    def head_at(k):
        return lax.rem(h + 2 * k + NH, NH)

    partner_y = dev(y + 1 - 2 * ylo, z, h)
    sibling = h + 1 - 2 * lax.rem(h, 2)
    right, left = dev(y, z, head_at(1)), dev(y, z, head_at(-1))
    core = dev(y, z, sibling)
    bits = (lax.rem(h, 2), lax.rem(h // 2, 2), h // 4)
    peers = []
    for i in range(1, NH):
        flips = (i & 1, (i >> 1) & 1, i >> 2)
        peers.append(
            sum((b + f - 2 * b * f) * w for b, f, w in zip(bits, flips, (1, 2, 4)))
        )

    count = [0]
    started = []

    def new(n=1):
        first = count[0]
        count[0] += n
        assert count[0] <= N_SEMS
        return first

    def copy(src, dst, device, recv=None, start=True):
        i = new()
        op = pltpu.make_async_remote_copy(
            src_ref=src,
            dst_ref=dst,
            send_sem=send_sem.at[i],
            recv_sem=recv_sem.at[i if recv is None else recv],
            device_id=device,
            device_id_type=MESH,
        )
        if start:
            op.start()
            started.append(op)
        return op

    my_head = head_of(z)
    piece = 4 * h + lax.rem(y + 4 - holder_shift(z), 4)
    own_piece = ylo * NZ + z
    w_targets = []
    for p in range(2):
        plane = head_of(2 * h + p)
        w_targets.append(
            dev(
                lax.rem(lax.rem(own_piece, 4) + holder_shift(plane), 4),
                plane,
                own_piece // 4,
            )
        )
    barrier = pltpu.get_barrier_semaphore()
    greet = [dev(y, z, j) for j in peers]
    greet += [at_z(k) for k in range(1, NZ)]
    greet += [at_y(1), at_y(-1)]
    greet += [(piece, my_head // 2, s) for s in range(2)]
    for d in greet:
        pl.semaphore_signal(barrier, inc=1, device_id=d, device_id_type=MESH)
    pl.semaphore_wait(barrier, len(greet))

    def rows(ref, start, size, unit):
        return ref.at[pl.ds(pl.multiple_of(start, unit), size)]

    tok_in = [
        copy(rows(tok, PART * j, PART, PART), ta.at[h], dev(y, z, j)) for j in peers
    ]
    ta[h] = tok[pl.ds(pl.multiple_of(PART * h, PART), PART), :]

    for p in range(2):
        for j in range(3):
            wp[p, :, j * HDIM : (j + 1) * HDIM] = w_in[
                :, j * 2 * HDIM + p * HDIM : j * 2 * HDIM + (p + 1) * HDIM
            ]
    w_recv = new(2)
    for p in range(2):
        copy(
            wp.at[p],
            rows(wb, 96 * own_piece + 48 * yhi, 48, 48),
            w_targets[p],
            recv=w_recv + yhi,
        )
    w_in_ops = [
        copy(
            wp.at[s],
            rows(wb, 96 * piece + 48 * s, 48, 48),
            core,
            recv=w_recv + s,
            start=False,
        )
        for s in range(2)
    ]

    wo_in = [
        copy(
            w_out.at[
                pl.ds(pl.multiple_of(64 * y, 64), 64),
                pl.ds(pl.multiple_of(FEAT * j, FEAT), FEAT),
            ],
            wo.at[h, y],
            dev(y, z, j),
        )
        for j in peers
    ]

    for op in tok_in:
        op.wait_recv()
    total = jnp.zeros((PART, 1), F32)
    for j in range(NH):
        total += jnp.sum(ta[j].astype(F32), axis=-1, keepdims=True)
    center = total / WIDTH
    total = jnp.zeros((PART, 1), F32)
    for j in range(NH):
        total += jnp.sum((ta[j].astype(F32) - center) ** 2, axis=-1, keepdims=True)
    scale = lax.rsqrt(total / WIDTH + 1e-06)
    for j in range(NH):
        cols = slice(FEAT * j, FEAT * (j + 1))
        normed = (ta[j].astype(F32) - center) * scale
        xb[0, :, cols] = (
            normed * (1.0 + mod[1:2, cols].astype(F32)) + mod[0:1, cols].astype(F32)
        ).astype(BF16)

    half = PART // 2

    def part(slot, i):
        return xb.at[slot, pl.ds(half * i, half)]

    from_left, from_right = {}, {}

    def ring_send(k):
        def one(i, rightward):
            if rightward:
                src = 0 if k == 1 else 2 * (k - 1) - 1
                dst = 2 * k - 1
            else:
                src = 0 if k == 1 else 2 * (k - 1)
                dst = 2 * k if k < 8 else 15
            op = copy(part(src, i), part(dst, i), at_z(1) if rightward else at_z(-1))
            (from_left if rightward else from_right)[k, i] = op

        if k < 8:
            for i in range(2):
                for rightward in (True, False):
                    if k > 1:
                        (from_left if rightward else from_right)[k - 1, i].wait_recv()
                    one(i, rightward)
        else:
            for i in range(2):
                from_left[7, i].wait_recv()
                if i == 0:
                    one(0, True)
                from_right[7, i].wait_recv()
                if i == 1:
                    one(1, False)

    ring_send(1)

    def project(b):
        x = xb[SLOTS * b : SLOTS * (b + 1)].reshape(ROWS, WIDTH)
        qkv = jnp.dot(x, wb[...], preferred_element_type=F32)

        def norm(v, gain):
            mean_square = jnp.mean(v * v, axis=-1, keepdims=True)
            return (v * lax.rsqrt(mean_square + 1e-06) * gain[...]).astype(BF16)

        qb[ROWS * b : ROWS * (b + 1), :] = norm(qkv[:, :HDIM], q_gain)
        mine = pl.ds(pl.multiple_of(ROWS * (2 * h + ylo), ROWS), ROWS)
        kv[b, mine, 0:HDIM] = norm(qkv[:, HDIM : 2 * HDIM], k_gain)
        kv[b, mine, HDIM : 2 * HDIM] = qkv[:, 2 * HDIM :].astype(BF16)

    def kv_rows(b, j, first=0, n=2):
        start = ROWS * (2 * j + first)
        return kv.at[b, pl.ds(pl.multiple_of(start, ROWS), ROWS * n)]

    kv_y, kv_l, kv_r, kv_fl, kv_fr, kv_c = {}, {}, {}, {}, {}, {}

    def kv_pair(b):
        kv_y[b] = copy(kv_rows(b, h, ylo, 1), kv_rows(b, h, ylo, 1), partner_y)

    def kv_own(b):
        kv_y[b].wait_recv()
        block = kv_rows(b, h)
        kv_l[b] = copy(block, block, right)
        kv_r[b] = copy(block, block, left)
        kv_c[b] = [copy(block, block, core)]

    def kv_forward(b):
        lh, rh = head_at(-1), head_at(1)
        kv_l[b].wait_recv()
        kv_fl[b] = copy(kv_rows(b, lh, 0, 1), kv_rows(b, lh, 0, 1), right)
        kv_c[b].append(copy(kv_rows(b, lh), kv_rows(b, lh), core))
        kv_r[b].wait_recv()
        kv_fr[b] = copy(kv_rows(b, rh, 1, 1), kv_rows(b, rh, 1, 1), left)
        kv_c[b].append(copy(kv_rows(b, rh), kv_rows(b, rh), core))

    def kv_last(b):
        kv_fl[b].wait_recv()
        kv_fr[b].wait_recv()
        far = kv_rows(b, head_at(2))
        kv_c[b].append(copy(far, far, core))

    def kv_done(b):
        for op in kv_c[b]:
            op.wait_recv()

    for op in w_in_ops:
        op.wait_recv()

    def w_rows(t, first=0, n=96):
        return rows(wb, 96 * t + first, n, 48)

    def w_piece(k):
        return 4 * h + lax.rem(piece + k + 4, 4)

    w_up = copy(w_rows(piece), w_rows(piece), at_y(1))
    w_down = copy(w_rows(piece), w_rows(piece), at_y(-1))

    ring_send(2)

    w_up.wait_recv()
    w_up2 = copy(w_rows(w_piece(-1), 0, 48), w_rows(w_piece(-1), 0, 48), at_y(1))
    w_down.wait_recv()
    w_down2 = copy(w_rows(w_piece(1), 48, 48), w_rows(w_piece(1), 48, 48), at_y(-1))

    ring_send(3)

    def w_block(j, first=0, n=384):
        return rows(wb, 384 * j + first, n, 192)

    w_up2.wait_recv()
    w_down2.wait_recv()
    w_l = copy(w_block(h), w_block(h), right)
    w_r = copy(w_block(h), w_block(h), left)
    w_c = [copy(w_block(h), w_block(h), core)]

    for op in wo_in:
        op.wait_recv()
    wo[h, y] = w_out[
        pl.ds(pl.multiple_of(64 * y, 64), 64),
        pl.ds(pl.multiple_of(FEAT * h, FEAT), FEAT),
    ]
    wo_up = copy(wo.at[:, y], wo.at[:, y], at_y(1))
    wo_down = copy(wo.at[:, y], wo.at[:, y], at_y(-1))

    ring_send(4)

    lh, rh = head_at(-1), head_at(1)
    w_l.wait_recv()
    w_fl = copy(w_block(lh, 0, 192), w_block(lh, 0, 192), right)
    w_c.append(copy(w_block(lh), w_block(lh), core))
    w_r.wait_recv()
    w_fr = copy(w_block(rh, 192, 192), w_block(rh, 192, 192), left)
    w_c.append(copy(w_block(rh), w_block(rh), core))

    ring_send(5)

    w_fl.wait_recv()
    w_fr.wait_recv()
    w_c.append(copy(w_block(head_at(2)), w_block(head_at(2)), core))
    for op in w_c:
        op.wait_recv()

    project(0)
    kv_pair(0)

    ring_send(6)

    project(1)
    kv_pair(1)
    kv_own(0)

    ring_send(7)

    project(2)
    kv_pair(2)
    kv_own(1)

    ring_send(8)

    kv_forward(0)
    y_up, y_down = lax.rem(y + 1, 4), lax.rem(y + 3, 4)
    wo_up.wait_recv()
    wo_up2 = copy(
        wo.at[pl.ds(0, 4), y_down], wo.at[pl.ds(0, 4), y_down], at_y(1)
    )
    wo_down.wait_recv()
    wo_down2 = copy(wo.at[pl.ds(4, 4), y_up], wo.at[pl.ds(4, 4), y_up], at_y(-1))
    kv_own(2)

    from_left[8, 0].wait_recv()
    from_right[8, 1].wait_recv()
    project(3)
    kv_pair(3)
    kv_forward(1)
    kv_last(0)
    kv_own(3)
    kv_forward(2)
    kv_last(1)
    kv_done(0)

    def attend(b):
        s = lax.dot_general(
            qb[...], kv[b, :, 0:HDIM], (((1,), (1,)), ((), ())), preferred_element_type=F32
        )
        top = jnp.max(s, axis=1, keepdims=True) * EXP2_SCALE
        if b > 0:
            before = m_s[...]
            now = jnp.maximum(before, top)
            factor = jnp.exp2(before - now)
        else:
            now = jnp.broadcast_to(top, (BATCHES * ROWS, HDIM))
        p = jnp.exp2(s * EXP2_SCALE - now[:, 0:1])
        o = jnp.dot(p.astype(BF16), kv[b, :, HDIM:], preferred_element_type=F32)
        t = jnp.sum(p, axis=1, keepdims=True)
        if b > 0:
            l_s[...] = l_s[...] * factor + t
            a_s[...] = a_s[...] * factor + o
        else:
            l_s[...] = jnp.broadcast_to(t, (BATCHES * ROWS, HDIM))
            a_s[...] = o
        m_s[...] = now

    attend(0)
    kv_forward(3)
    kv_last(2)
    kv_done(1)
    attend(1)
    kv_last(3)
    kv_done(2)
    attend(2)
    kv_done(3)
    attend(3)

    os[...] = (a_s[...] / l_s[...]).astype(BF16).reshape(NZ, PART, HDIM)

    mine = pl.ds(pl.multiple_of(HDIM * my_head, HDIM), HDIM)
    back = []
    for k in range(1, 8):
        back.append(copy(os.at[2 * k - 1], ob.at[h, :, mine], at_z(-k)))
        back.append(copy(os.at[2 * k], ob.at[h, :, mine], at_z(k)))
    back.append(copy(os.at[15], ob.at[h, :, mine], at_z(8)))
    ob[h, :, mine] = os[0]
    wo_up2.wait_recv()
    wo_down2.wait_recv()
    for op in back:
        op.wait_recv()

    def o_block(j, first=0, n=PART):
        return ob.at[j, pl.ds(first, n)]

    o_l = copy(o_block(h), o_block(h), right)
    o_r = copy(o_block(h), o_block(h), left)
    o_c = [copy(o_block(h), o_block(h), core)]
    o_l.wait_recv()
    o_fl = copy(o_block(lh, 0, 16), o_block(lh, 0, 16), right)
    o_c.append(copy(o_block(lh), o_block(lh), core))
    o_r.wait_recv()
    o_fr = copy(o_block(rh, 16, 16), o_block(rh, 16, 16), left)
    o_c.append(copy(o_block(rh), o_block(rh), core))
    o_fl.wait_recv()
    o_fr.wait_recv()
    far = head_at(2)
    o_c.append(copy(o_block(far), o_block(far), core))
    for op in o_c:
        op.wait_recv()

    projected = jnp.dot(
        ob[...].reshape(TOK, 2048),
        wo[...].reshape(2048, FEAT),
        preferred_element_type=F32,
    )
    gate = mod[2:3, pl.ds(pl.multiple_of(FEAT * h, FEAT), FEAT)].astype(F32)
    out[...] = (gate * projected).astype(BF16)

    for op in started:
        op.wait_send()


def body(tokens, modulation, w_qkv, query_gain, key_gain, w_out):
    vmem = pl.BlockSpec(memory_space=pltpu.VMEM)
    branch = pl.pallas_call(
        kernel,
        out_shape=jax.ShapeDtypeStruct((TOK, FEAT), BF16),
        in_specs=[vmem] * 6,
        out_specs=vmem,
        scratch_shapes=[
            pltpu.VMEM((2, 48, QKV), BF16),
            pltpu.VMEM((NH, PART, FEAT), BF16),
            pltpu.VMEM((NZ, PART, WIDTH), BF16),
            pltpu.VMEM((WIDTH, QKV), BF16),
            pltpu.VMEM((BATCHES * ROWS, HDIM), BF16),
            pltpu.VMEM((BATCHES, 16 * ROWS, 2 * HDIM), BF16),
            pltpu.VMEM((NH, 4, 64, FEAT), BF16),
            pltpu.VMEM((NZ, PART, HDIM), BF16),
            pltpu.VMEM((NH, PART, 2048), BF16),
            pltpu.VMEM((BATCHES * ROWS, HDIM), F32),
            pltpu.VMEM((BATCHES * ROWS, HDIM), F32),
            pltpu.VMEM((BATCHES * ROWS, HDIM), F32),
            pltpu.SemaphoreType.DMA((N_SEMS,)),
            pltpu.SemaphoreType.DMA((N_SEMS,)),
        ],
        compiler_params=pltpu.CompilerParams(
            collective_id=0, has_side_effects=True, vmem_limit_bytes=48 << 20
        ),
        name="branch",
    )(
        tokens[0],
        modulation[0],
        w_qkv.reshape(48, 6 * HDIM),
        query_gain.reshape(1, HDIM),
        key_gain.reshape(1, HDIM),
        w_out,
    )
    return branch[None]


def solution(mesh):
    in_specs = (
        P("grp", "ctx", "head"),
        P("grp", None, None),
        P(("ctx", "grp"), None, "head"),
        P(),
        P(),
        P("head", None),
    )
    out_specs = P("grp", "ctx", "head")
    return jax.shard_map(body, mesh=mesh, in_specs=in_specs, out_specs=out_specs, check_vma=False)
```

```python
import functools

import jax
import jax.numpy as jnp
import numpy as np
from jax import lax
from jax.experimental import pallas as pl
from jax.experimental.pallas import tpu as pltpu
from jax.sharding import PartitionSpec as P

MESH = pl.DeviceIdType.MESH
BF16 = jnp.bfloat16
F32 = jnp.float32
NZ, NH, HDIM = 16, 8, 128
TOK, FEAT, WIDTH = 256, 384, 3072
PART = 32
SPLIT = (4, 4, 4, 3, 1)
FIRST = tuple(sum(SPLIT[:b]) for b in range(len(SPLIT)))
LAST = len(SPLIT) - 1
ROWS = NZ * PART
HALF = PART // 2
EARLY = ((0, 1), (1, 1))
LATE = ((2, 1), (3, 2))
N_SEMS = 240
WAYS = (1, 3, 2)
(
    W_SENT, W_HERE, TOKENS, W_OUT, BLOCK, W_A_Y, W_B_X, W_A_X, W_B_Y, W_CORE,
    KV_BLOCK, KV_CORE, W_OUT_Y, ATTENDED, HEADS, HEADS_CORE,
) = range(16)
(
    W1, SPREAD, WO, LN, RING, WD, WFA, WFB, WC, PROJ, KVF, KVC, WOY, EA, LA, BACK, O, OC, OUT,
) = range(19)
EXP2_SCALE = float(HDIM ** (-0.5) * np.log2(np.e))
ORDER = (
    (W1,), (SPREAD,), (LN,), (WO,), (RING, 2, 1, 0), (RING, 2, 0, 0), (WD,), (RING, 2, 1, 1),
    (RING, 2, 0, 1), (RING, 2, 0, 2), (RING, 2, 1, 2), (RING, 2, 0, 3), (RING, 2, 1, 3),
    (RING, 3, 0, 0), (WFA, 1), (RING, 3, 1, 0), (WFB, 3), (WFB, 1), (RING, 3, 0, 1),
    (RING, 3, 1, 1), (WFA, 3), (WFB, 2), (RING, 3, 0, 2), (RING, 3, 1, 2), (RING, 3, 0, 3),
    (WFA, 2), (RING, 3, 1, 3), (RING, 4, 0, 0), (RING, 4, 1, 0), (RING, 4, 1, 1),
    (RING, 4, 0, 1), (WC, 0), (RING, 4, 0, 2), (RING, 4, 1, 2), (WC, 3), (RING, 4, 0, 3),
    (WC, 1), (RING, 4, 1, 3), (RING, 5, 1, 0), (RING, 5, 0, 0), (WC, 2), (RING, 5, 0, 1),
    (RING, 5, 1, 1), (RING, 5, 0, 2), (RING, 5, 1, 2), (PROJ, 0), (RING, 5, 0, 3),
    (RING, 5, 1, 3), (PROJ, 1), (RING, 6, 0, 0), (RING, 6, 1, 0), (RING, 6, 0, 1),
    (RING, 6, 1, 1), (RING, 6, 0, 2), (RING, 6, 1, 2), (RING, 6, 0, 3), (RING, 6, 1, 3),
    (KVF, 0), (RING, 7, 0, 0), (RING, 7, 1, 0), (RING, 7, 1, 1), (RING, 7, 0, 1),
    (RING, 7, 1, 2), (KVF, 1), (RING, 7, 0, 2), (RING, 7, 1, 3), (RING, 7, 0, 3), (PROJ, 2),
    (RING, 8, 0, 0), (KVC, 0, 1), (KVC, 0, 3), (RING, 8, 0, 1), (RING, 8, 1, 2), (KVC, 0, 2),
    (KVC, 1, 3), (RING, 8, 1, 3), (KVF, 2), (PROJ, 3), (KVC, 1, 2), (EA, 0, 0), (KVC, 1, 1),
    (PROJ, 4), (EA, 1, 0), (KVF, 3), (KVC, 2, 1), (KVC, 2, 3), (EA, 1, 1), (KVC, 2, 2),
    (EA, 0, 1), (WOY,), (KVC, 4, 0), (KVC, 4, 1), (KVC, 4, 3), (KVC, 4, 2), (KVC, 3, 1),
    (KVC, 3, 3), (LA, 0, 0), (KVC, 3, 2), (LA, 1, 0), (LA, 0, 1), (BACK, 0), (LA, 1, 1),
    (BACK, 1), (O, 0), (O, 1), (OC, 0, 1), (OC, 0, 3), (OC, 0, 2), (OC, 1, 1), (OC, 1, 3),
    (OC, 1, 2), (OUT,),
)


def head_of(z):
    return lax.rem(z, 4) * 4 + z // 4


def kernel(
    tok,
    mod_hbm,
    w_in,
    q_gain_hbm,
    k_gain_hbm,
    w_out,
    out,
    mod,
    q_gain,
    k_gain,
    wp,
    ta,
    xb,
    wb,
    qb,
    kv,
    wo,
    os,
    ob,
    m_s,
    l_s,
    a_s,
    local_sem,
    send_sem,
    recv_sem,
):
    c = lax.axis_index("ctx")
    h = lax.axis_index("head")
    yhi = lax.axis_index("grp")
    ylo, z = c // NZ, lax.rem(c, NZ)
    y = 2 * yhi + ylo

    def dev(y, z, h):
        return (lax.rem(y, 2) * NZ + z, h, y // 2)

    def at_z(k):
        return dev(y, lax.rem(z + k + NZ, NZ), h)

    def at_y(k):
        return dev(lax.rem(y + k + 4, 4), z, h)

    def head_at(k):
        return lax.rem(h + 2 * k + NH, NH)

    def at(dx, dy):
        return dev(lax.rem(y + dy, 4), z, head_at(dx))

    other_y = y + 1 - 2 * ylo
    core = dev(y, z, h + 1 - 2 * lax.rem(h, 2))
    bits = (lax.rem(h, 2), lax.rem(h // 2, 2), h // 4)
    peers = []
    for i in range(NH):
        flips = (i & 1, (i >> 1) & 1, i >> 2)
        peers.append(
            sum((b + f - 2 * b * f) * w for b, f, w in zip(bits, flips, (1, 2, 4)))
        )

    count = [0]
    started = []
    ops = {}

    def copy(name, src, dst, device, recv=None, start=True):
        i = count[0]
        count[0] += 1
        assert i < N_SEMS
        op = pltpu.make_async_remote_copy(
            src_ref=src,
            dst_ref=dst,
            send_sem=send_sem.at[i],
            recv_sem=recv_sem.at[i if recv is None else recv],
            device_id=device,
            device_id_type=MESH,
        )
        if start:
            op.start()
            started.append(op)
        assert name not in ops
        ops[name] = op

    waited = set()

    def wait(*names):
        for name in names:
            if name not in waited:
                waited.add(name)
                ops[name].wait_recv()

    def rows(ref, start, size, unit):
        return ref.at[pl.ds(pl.multiple_of(start, unit), size)]

    def span(start, size):
        return pl.ds(pl.multiple_of(start, size), size)

    my_head = head_of(z)
    piece = lax.rem(h + 4, NH)
    w_targets = [
        dev(y, head_of(2 * h + p), lax.rem(z // 2 + 4, NH)) for p in range(2)
    ]

    locals_ = []

    def local(src, dst):
        op = pltpu.make_async_copy(src, dst, local_sem.at[len(locals_)])
        op.start()
        locals_.append(op)
        return op

    wp_ops = [
        local(
            w_in.at[j, :, pl.ds(p * HDIM, HDIM)],
            wp.at[p, :, pl.ds(j * HDIM, HDIM)],
        )
        for p in range(2)
        for j in range(3)
    ]
    tok_own = local(rows(tok, PART * h, PART, PART), ta.at[h])
    mod_op = local(mod_hbm, mod)
    gain_ops = [local(q_gain_hbm, q_gain), local(k_gain_hbm, k_gain)]
    wo_own = local(w_out.at[span(64 * y, 64), span(FEAT * h, FEAT)], wo.at[h, y])

    barrier = pltpu.get_barrier_semaphore()
    greet = [dev(y, z, peers[i]) for i in range(1, NH)]
    greet += [at_z(k) for k in range(1, NZ)]
    greet += [at(dx, dy) for dx in range(4) for dy in WAYS]
    greet += [dev(y, 2 * piece + s, my_head // 2) for s in range(2)]
    for d in greet:
        pl.semaphore_signal(barrier, inc=1, device_id=d, device_id_type=MESH)
    pl.semaphore_wait(barrier, len(greet))

    tasks = {}

    def task(*name):
        def add(f):
            tasks[name] = f
            return f

        return add

    @task(W1)
    def _():
        for op in wp_ops:
            op.wait()
        base = count[0]
        for p in range(2):
            copy(
                (W_SENT, p),
                wp.at[p],
                wb.at[ylo, z // 2, lax.rem(z, 2), yhi],
                w_targets[p],
                recv=base + lax.rem(z, 2),
            )
        for s in range(2):
            copy(
                (W_HERE, s),
                wp.at[s],
                wb.at[ylo, piece, s, yhi],
                core,
                recv=base + s,
                start=False,
            )

    def w_half(dx, dy, s):
        yy = lax.rem(y + dy, 4)
        return wb.at[lax.rem(yy, 2), lax.rem(head_at(dx) + 4, NH), s, yy // 2]

    def w_send(name, block, dx, dy):
        copy(name, block, block, at(dx, dy))

    @task(WD)
    def _():
        wait((W_HERE, 0), (W_HERE, 1))
        for d in WAYS:
            w_send((W_A_Y, 4 - d), w_half(0, 0, 0), 0, d)
        for d in WAYS:
            w_send((W_B_X, 4 - d), w_half(0, 0, 1), d, 0)
        for d in WAYS:
            w_send((W_A_X, 4 - d, 0), w_half(0, 0, 0), d, 0)
        for d in WAYS:
            w_send((W_B_Y, 0, 4 - d), w_half(0, 0, 1), 0, d)

    def add_w_forward(d):
        @task(WFA, d)
        def _():
            wait((W_A_Y, d))
            for dx in WAYS:
                w_send((W_A_X, 4 - dx, d), w_half(0, d, 0), dx, 0)

        @task(WFB, d)
        def _():
            wait((W_B_X, d))
            for dy in WAYS:
                w_send((W_B_Y, d, 4 - dy), w_half(d, 0, 1), 0, dy)

    for d in WAYS:
        add_w_forward(d)

    def w_names(dx):
        if dx == 0:
            names = [(W_A_Y, dy) for dy in WAYS]
        else:
            names = [(W_B_X, dx)] + [(W_A_X, dx, dy) for dy in range(4)]
        return names + [(W_B_Y, dx, dy) for dy in WAYS]

    def add_w_core(dx):
        @task(WC, dx)
        def _():
            wait(*w_names(dx))
            block = wb.at[:, lax.rem(head_at(dx) + 4, NH)]
            copy((W_CORE, dx), block, block, core)

    for dx in range(4):
        add_w_core(dx)

    @task(SPREAD)
    def _():
        for i in range(1, NH):
            copy(
                (TOKENS, i),
                rows(tok, PART * peers[i], PART, PART),
                ta.at[h],
                dev(y, z, peers[i]),
            )

    @task(WO)
    def _():
        for i in range(1, NH):
            copy(
                (W_OUT, i),
                w_out.at[span(64 * y, 64), span(FEAT * peers[i], FEAT)],
                wo.at[h, y],
                dev(y, z, peers[i]),
            )

    @task(LN)
    def _():
        wait(*((TOKENS, i) for i in range(1, NH)))
        tok_own.wait()
        mod_op.wait()
        total = jnp.zeros((PART, 1), F32)
        for j in range(NH):
            total += jnp.sum(ta[j].astype(F32), axis=-1, keepdims=True)
        center = total / WIDTH
        total = jnp.zeros((PART, 1), F32)
        for j in range(NH):
            total += jnp.sum((ta[j].astype(F32) - center) ** 2, axis=-1, keepdims=True)
        scale = lax.rsqrt(total / WIDTH + 1e-06)
        for j in range(NH):
            cols = slice(FEAT * j, FEAT * (j + 1))
            normed = (ta[j].astype(F32) - center) * scale
            xb[0, :, cols] = (
                normed * (1.0 + mod[1:2, cols].astype(F32)) + mod[0:1, cols].astype(F32)
            ).astype(BF16)
        for i in range(4):
            ring_copy(1, 0, i)
            ring_copy(1, 1, i)

    def ring_copy(k, way, i):
        step = min(2 * k - 1 + way, 15)
        before = 0 if k == 1 else 2 * k - 3 + way
        half = pl.ds(PART // 2 * (i // 2), PART // 2)
        cols = pl.ds(WIDTH // 2 * (i % 2), WIDTH // 2)
        copy(
            (BLOCK, way, k, i),
            xb.at[before, half, cols],
            xb.at[step, half, cols],
            at_z(1 - 2 * way),
        )

    def add_ring(k, way, i):
        @task(RING, k, way, i)
        def _():
            wait((BLOCK, way, k - 1, i))
            ring_copy(k, way, i)

    for k in range(2, 9):
        for way in range(2):
            for i in range(4):
                if k < 8 or (way == 0) == (i < 2):
                    add_ring(k, way, i)

    def slot_names(s):
        if s == 0:
            return []
        if s == 15:
            return [(BLOCK, 0, 8, 0), (BLOCK, 0, 8, 1), (BLOCK, 1, 8, 2), (BLOCK, 1, 8, 3)]
        way, k = 1 - s % 2, (s + 1) // 2
        return [(BLOCK, way, k, i) for i in range(4)]

    @task(WOY)
    def _():
        wait(*((W_OUT, i) for i in range(1, NH)))
        wo_own.wait()
        for dy in WAYS:
            copy((W_OUT_Y, dy), wo.at[:, y], wo.at[:, y], at(0, dy))

    def kv_slot(b, j, yl):
        n = PART * SPLIT[b]
        return pl.ds(pl.multiple_of(NZ * PART * FIRST[b] + n * (2 * j + yl), PART), n)

    def add_batch(b):
        first, n = PART * FIRST[b], PART * SPLIT[b]

        def norm(v, gain):
            mean_square = jnp.mean(v * v, axis=-1, keepdims=True)
            return (v * lax.rsqrt(mean_square + 1e-06) * gain[...]).astype(BF16)

        @task(PROJ, b)
        def _():
            for dx in range(4):
                wait(*w_names(dx), (W_CORE, dx))
            for s in range(FIRST[b], FIRST[b] + SPLIT[b]):
                wait(*slot_names(s))
            if b == 0:
                for op in gain_ops:
                    op.wait()
            x = xb[FIRST[b] : FIRST[b] + SPLIT[b]].reshape(n, WIDTH)
            w = wb[...].reshape(WIDTH, 3 * HDIM)
            qkv = jnp.dot(x, w, preferred_element_type=F32)
            here = kv_slot(b, h, ylo)
            kv[here, 0:HDIM] = norm(qkv[:, HDIM : 2 * HDIM], k_gain)
            kv[here, HDIM : 2 * HDIM] = qkv[:, 2 * HDIM :].astype(BF16)
            mine = kv.at[here]
            qs = norm(qkv[:, :HDIM], q_gain).reshape(SPLIT[b], 2, HALF, HDIM)
            for yy in range(2 if b == LAST else 1):
                for dx in (0,) + WAYS:
                    if dx or yy:
                        there = dev(other_y if yy else y, z, head_at(dx))
                        copy((KV_BLOCK, b, (4 - dx) % 4, yy), mine, mine, there)
            if b < LAST:
                copy((KV_BLOCK, b, 0, 1), mine, mine, dev(other_y, z, h))
            for i in range(2):
                qb[i, HALF * FIRST[b] : HALF * (FIRST[b] + SPLIT[b])] = qs[:, i].reshape(
                    n // 2, HDIM
                )

        def pair(dx):
            start = NZ * first + 2 * n * head_at(dx)
            return rows(kv, start, 2 * n, PART)

        if b < LAST:

            @task(KVF, b)
            def _():
                wait((KV_BLOCK, b, 0, 1))
                block = kv.at[kv_slot(b, h, 1 - ylo)]
                for dx in WAYS:
                    copy((KV_BLOCK, b, 4 - dx, 1), block, block, at(dx, 0))
                copy((KV_CORE, b, 0), pair(0), pair(0), core)

        def add_core(dx):
            @task(KVC, b, dx)
            def _():
                wait(*((KV_BLOCK, b, dx, yy) for yy in range(2) if dx or yy))
                copy((KV_CORE, b, dx), pair(dx), pair(dx), core)

        for dx in WAYS if b < LAST else range(4):
            add_core(dx)

    for b in range(LAST + 1):
        add_batch(b)

    def kv_names(b):
        names = [(KV_BLOCK, b, dx, yy) for dx in range(4) for yy in range(2) if dx or yy]
        return names + [(KV_CORE, b, dx) for dx in range(4)]

    def attend(batches, where, start, end):
        b, n = batches
        for i in range(n):
            wait(*kv_names(b + i))
        keys = pl.ds(NZ * PART * FIRST[b], NZ * PART * sum(SPLIT[b : b + n]))

        def get(ref):
            return ref[where].reshape(ROWS // 2, HDIM)

        def put(ref, value):
            ref[where] = value.reshape(ref[where].shape)

        s = lax.dot_general(
            get(qb),
            kv[keys, 0:HDIM],
            (((1,), (1,)), ((), ())),
            preferred_element_type=F32,
        )
        top = jnp.max(s, axis=1, keepdims=True) * EXP2_SCALE
        if start:
            now = jnp.broadcast_to(top, (ROWS // 2, HDIM))
        else:
            before = get(m_s)
            now = jnp.maximum(before, top)
            factor = jnp.exp2(before - now)
        p = jnp.exp2(s * EXP2_SCALE - now[:, 0:1])
        o = jnp.dot(p.astype(BF16), kv[keys, HDIM:], preferred_element_type=F32)
        t = jnp.broadcast_to(jnp.sum(p, axis=1, keepdims=True), (ROWS // 2, HDIM))
        if not start:
            t += get(l_s) * factor
            o += get(a_s) * factor
        if end:
            put(os, (o / t).astype(BF16))
        else:
            put(m_s, now)
            put(l_s, t)
            put(a_s, o)

    def add_attention(g, j, early):
        @task(EA if early else LA, g, j)
        def _():
            if early:
                slots = slice(ROWS // 4 * g, ROWS // 4 * (g + 1))
                attend(EARLY[j], (slice(None), slots), j == 0, False)
            else:
                attend(LATE[j], g, not EARLY and j == 0, j == len(LATE) - 1)

    for g in range(2):
        for j in range(len(EARLY)):
            add_attention(g, j, True)
        for j in range(len(LATE)):
            add_attention(g, j, False)

    head_cols = span(HDIM * my_head, HDIM)

    def add_return(g):
        half = pl.ds(HALF * g, HALF)

        @task(BACK, g)
        def _():
            for s in reversed(range(NZ)):
                here = os.at[g, pl.ds(HALF * s, HALF)]
                if s == 0:
                    ob[h, half, head_cols] = os[g, 0:HALF]
                    continue
                k = 8 if s == 15 else (-((s + 1) // 2) if s % 2 else s // 2)
                copy((ATTENDED, g, s), here, ob.at[h, half, head_cols], at_z(k))

        @task(O, g)
        def _():
            wait(*((ATTENDED, g, s) for s in range(1, NZ)))
            block = ob.at[h, half]
            copy((HEADS_CORE, g, 0), block, block, core)
            for dx in WAYS:
                copy((HEADS, g, 4 - dx), block, block, at(dx, 0))

        def add_core(dx):
            @task(OC, g, dx)
            def _():
                wait((HEADS, g, dx))
                block = ob.at[head_at(dx), half]
                copy((HEADS_CORE, g, dx), block, block, core)

        for dx in WAYS:
            add_core(dx)

    for g in range(2):
        add_return(g)

    @task(OUT)
    def _():
        wait(*((W_OUT_Y, dy) for dy in WAYS))
        wait(*((HEADS_CORE, g, dx) for g in range(2) for dx in range(4)))
        projected = jnp.dot(
            ob[...].reshape(TOK, 2048),
            wo[...].reshape(2048, FEAT),
            preferred_element_type=F32,
        )
        gate = mod[2:3, span(FEAT * h, FEAT)].astype(F32)
        out[...] = (gate * projected).astype(BF16)

    assert set(ORDER) == set(tasks) and len(ORDER) == len(tasks)
    for name in ORDER:
        tasks[name]()
    for op in started:
        op.wait_send()


def body(tokens, modulation, w_qkv, query_gain, key_gain, w_out):
    branch = pl.pallas_call(
        kernel,
        out_shape=jax.ShapeDtypeStruct((TOK, FEAT), BF16),
        in_specs=[pl.BlockSpec(memory_space=pltpu.HBM)] * 6,
        out_specs=pl.BlockSpec(memory_space=pltpu.VMEM),
        scratch_shapes=[
            pltpu.VMEM((3, WIDTH), BF16),
            pltpu.VMEM((1, HDIM), F32),
            pltpu.VMEM((1, HDIM), F32),
            pltpu.VMEM((2, 48, 3 * HDIM), BF16),
            pltpu.VMEM((NH, PART, FEAT), BF16),
            pltpu.VMEM((NZ, PART, WIDTH), BF16),
            pltpu.VMEM((2, NH, 2, 2, 48, 3 * HDIM), BF16),
            pltpu.VMEM((2, ROWS // 2, HDIM), BF16),
            pltpu.VMEM((NZ * ROWS, 2 * HDIM), BF16),
            pltpu.VMEM((NH, 4, 64, FEAT), BF16),
            pltpu.VMEM((2, ROWS // 2, HDIM), BF16),
            pltpu.VMEM((NH, PART, 2048), BF16),
            pltpu.VMEM((2, ROWS // 2, HDIM), F32),
            pltpu.VMEM((2, ROWS // 2, HDIM), F32),
            pltpu.VMEM((2, ROWS // 2, HDIM), F32),
            pltpu.SemaphoreType.DMA((16,)),
            pltpu.SemaphoreType.DMA((N_SEMS,)),
            pltpu.SemaphoreType.DMA((N_SEMS,)),
        ],
        compiler_params=pltpu.CompilerParams(
            collective_id=0, has_side_effects=True, vmem_limit_bytes=60 << 20
        ),
        name="branch",
    )(
        tokens[0],
        modulation[0],
        w_qkv.transpose(1, 0, 2),
        query_gain.reshape(1, HDIM),
        key_gain.reshape(1, HDIM),
        w_out,
    )
    return branch[None]


def solution(mesh):
    in_specs = (
        P("grp", "ctx", "head"),
        P("grp", None, None),
        P(("ctx", "grp"), None, "head"),
        P(),
        P(),
        P("head", None),
    )
    out_specs = P("grp", "ctx", "head")
    return jax.shard_map(body, mesh=mesh, in_specs=in_specs, out_specs=out_specs, check_vma=False)
```

```python
import functools

import jax
import jax.numpy as jnp
import numpy as np
from jax import lax
from jax.experimental import pallas as pl
from jax.experimental.pallas import tpu as pltpu
from jax.sharding import PartitionSpec as P

MESH = pl.DeviceIdType.MESH
BF16 = jnp.bfloat16
F32 = jnp.float32
NZ, NH, HDIM = 16, 8, 128
TOK, FEAT, WIDTH = 256, 384, 3072
PART = 32
SPLIT = (4, 4, 4, 3, 1)
FIRST = tuple(sum(SPLIT[:b]) for b in range(len(SPLIT)))
LAST = len(SPLIT) - 1
Y_FIRST, X_FIRST, STRAIGHT = range(3)
WAY_OF = (X_FIRST, Y_FIRST, STRAIGHT, STRAIGHT, STRAIGHT)
ROWS = NZ * PART
HALF = PART // 2
EARLY = ((0, 1), (1, 1), (2, 1))
LATE = ((3, 2),)
N_SEMS = 240
WAYS = (1, 3, 2)
(
    W_SENT, W_HERE, TOKENS, W_OUT, BLOCK, W_A_Y, W_B_X, W_A_X, W_B_Y, W_CORE,
    KV_BLOCK, KV_CORE, W_OUT_Y, ATTENDED, HEADS, HEADS_CORE,
) = range(16)
(
    W1, SPREAD, WO, LN, RING, WD, WFA, WFB, WC, PROJ, KVF, KVC, WOY, EA, LA, BACK, O, OC, OUT,
) = range(19)
EXP2_SCALE = float(HDIM ** (-0.5) * np.log2(np.e))
ORDER = (
    (W1,), (SPREAD,), (WO,), (LN,), (RING, 2, 0, 0), (RING, 2, 1, 0), (WD,), (RING, 2, 0, 1),
    (RING, 2, 1, 1), (RING, 2, 0, 2), (RING, 2, 1, 2), (RING, 2, 0, 3), (RING, 2, 1, 3),
    (WFA, 1), (WFB, 1), (WFA, 3), (WFB, 3), (RING, 3, 0, 0), (RING, 3, 1, 0), (RING, 3, 0, 1),
    (RING, 3, 1, 1), (WFA, 2), (WFB, 2), (RING, 3, 0, 2), (RING, 3, 1, 2), (WC, 0),
    (RING, 3, 0, 3), (RING, 3, 1, 3), (RING, 4, 0, 0), (RING, 4, 1, 0), (RING, 4, 0, 1),
    (RING, 4, 1, 1), (RING, 4, 0, 2), (RING, 4, 1, 2), (WC, 1), (WC, 3), (RING, 4, 0, 3),
    (RING, 4, 1, 3), (WC, 2), (RING, 5, 0, 0), (RING, 5, 1, 0), (RING, 5, 0, 1),
    (RING, 5, 1, 1), (PROJ, 0), (RING, 5, 0, 2), (RING, 5, 1, 2), (RING, 5, 0, 3),
    (RING, 5, 1, 3), (PROJ, 1), (RING, 6, 0, 0), (RING, 6, 1, 0), (RING, 6, 0, 1),
    (RING, 6, 1, 1), (KVF, 0, 1), (KVF, 0, 3), (KVC, 0, 0), (RING, 6, 0, 2), (RING, 6, 1, 2),
    (RING, 6, 0, 3), (KVF, 1, 0), (RING, 6, 1, 3), (RING, 7, 0, 0), (RING, 7, 1, 0),
    (KVF, 0, 2), (KVC, 0, 1), (RING, 7, 0, 1), (RING, 7, 1, 1), (RING, 7, 0, 2),
    (RING, 7, 1, 2), (PROJ, 2), (KVC, 0, 3), (RING, 8, 0, 0), (KVC, 1, 3), (RING, 7, 1, 3),
    (KVC, 0, 2), (KVC, 1, 1), (RING, 7, 0, 3), (KVC, 1, 2), (RING, 8, 0, 1), (RING, 8, 1, 2),
    (EA, 0, 0), (RING, 8, 1, 3), (PROJ, 3), (KVC, 2, 0), (EA, 0, 1), (KVC, 2, 1), (PROJ, 4),
    (KVC, 2, 3), (KVC, 2, 2), (KVC, 3, 0), (WOY,), (EA, 1, 0), (EA, 0, 2), (KVC, 4, 0),
    (KVC, 3, 1), (KVC, 3, 3), (EA, 1, 1), (KVC, 3, 2), (KVC, 4, 1), (KVC, 4, 3), (KVC, 4, 2),
    (EA, 1, 2), (LA, 0, 0), (BACK, 0), (LA, 1, 0), (BACK, 1), (O, 0), (O, 1), (OC, 0, 1),
    (OC, 0, 3), (OC, 0, 2), (OC, 1, 1), (OC, 1, 3), (OUT, 0), (OC, 1, 2), (OUT, 1),
)


def head_of(z):
    return lax.rem(z, 4) * 4 + z // 4


def kernel(
    tok,
    mod_hbm,
    w_in,
    q_gain_hbm,
    k_gain_hbm,
    w_out,
    out,
    mod,
    q_gain,
    k_gain,
    wp,
    ta,
    xb,
    wb,
    qb,
    kv,
    wo,
    os,
    ob,
    m_s,
    l_s,
    a_s,
    local_sem,
    send_sem,
    recv_sem,
):
    c = lax.axis_index("ctx")
    h = lax.axis_index("head")
    yhi = lax.axis_index("grp")
    ylo, z = c // NZ, lax.rem(c, NZ)
    y = 2 * yhi + ylo

    def dev(y, z, h):
        return (lax.rem(y, 2) * NZ + z, h, y // 2)

    def at_z(k):
        return dev(y, lax.rem(z + k + NZ, NZ), h)

    def at_y(k):
        return dev(lax.rem(y + k + 4, 4), z, h)

    def head_at(k):
        return lax.rem(h + 2 * k + NH, NH)

    def at(dx, dy):
        return dev(lax.rem(y + dy, 4), z, head_at(dx))

    other_y = y + 1 - 2 * ylo
    core = dev(y, z, h + 1 - 2 * lax.rem(h, 2))
    bits = (lax.rem(h, 2), lax.rem(h // 2, 2), h // 4)
    peers = []
    for i in range(NH):
        flips = (i & 1, (i >> 1) & 1, i >> 2)
        peers.append(
            sum((b + f - 2 * b * f) * w for b, f, w in zip(bits, flips, (1, 2, 4)))
        )

    count = [0]
    started = []
    ops = {}

    def copy(name, src, dst, device, recv=None, start=True):
        i = count[0]
        count[0] += 1
        assert i < N_SEMS
        op = pltpu.make_async_remote_copy(
            src_ref=src,
            dst_ref=dst,
            send_sem=send_sem.at[i],
            recv_sem=recv_sem.at[i if recv is None else recv],
            device_id=device,
            device_id_type=MESH,
        )
        if start:
            op.start()
            started.append((name, op))
        assert name not in ops
        ops[name] = op

    def drain(*later):
        for name, op in started:
            if name[0] not in later:
                op.wait_send()
        started[:] = [sent for sent in started if sent[0][0] in later]

    waited = set()

    def wait(*names):
        for name in names:
            if name not in waited:
                waited.add(name)
                ops[name].wait_recv()

    def rows(ref, start, size, unit):
        return ref.at[pl.ds(pl.multiple_of(start, unit), size)]

    def span(start, size):
        return pl.ds(pl.multiple_of(start, size), size)

    my_head = head_of(z)
    piece = lax.rem(h + 4, NH)
    w_targets = [
        dev(y, head_of(2 * h + p), lax.rem(z // 2 + 4, NH)) for p in range(2)
    ]

    locals_ = []

    def local(src, dst):
        op = pltpu.make_async_copy(src, dst, local_sem.at[len(locals_)])
        op.start()
        locals_.append(op)
        return op

    wp_ops = [
        local(
            w_in.at[j, :, pl.ds(p * HDIM, HDIM)],
            wp.at[p, :, pl.ds(j * HDIM, HDIM)],
        )
        for p in range(2)
        for j in range(3)
    ]
    tok_own = local(rows(tok, PART * h, PART, PART), ta.at[h])
    mod_op = local(mod_hbm, mod)
    gain_ops = [local(q_gain_hbm, q_gain), local(k_gain_hbm, k_gain)]
    wo_own = local(w_out.at[span(64 * y, 64), span(FEAT * h, FEAT)], wo.at[h, y])

    barrier = pltpu.get_barrier_semaphore()
    greet = [dev(y, z, peers[i]) for i in range(1, NH)]
    greet += [at_z(k) for k in range(1, NZ)]
    greet += [at(dx, dy) for dx in range(4) for dy in WAYS]
    greet += [dev(y, 2 * piece + s, my_head // 2) for s in range(2)]
    for d in greet:
        pl.semaphore_signal(barrier, inc=1, device_id=d, device_id_type=MESH)
    pl.semaphore_wait(barrier, len(greet))

    tasks = {}

    def task(*name):
        def add(f):
            tasks[name] = f
            return f

        return add

    @task(W1)
    def _():
        for op in wp_ops:
            op.wait()
        base = count[0]
        for p in range(2):
            copy(
                (W_SENT, p),
                wp.at[p],
                wb.at[ylo, z // 2, lax.rem(z, 2), yhi],
                w_targets[p],
                recv=base + lax.rem(z, 2),
            )
        for s in range(2):
            copy(
                (W_HERE, s),
                wp.at[s],
                wb.at[ylo, piece, s, yhi],
                core,
                recv=base + s,
                start=False,
            )

    def w_half(dx, dy, s):
        yy = lax.rem(y + dy, 4)
        return wb.at[lax.rem(yy, 2), lax.rem(head_at(dx) + 4, NH), s, yy // 2]

    def w_send(name, block, dx, dy):
        copy(name, block, block, at(dx, dy))

    @task(WD)
    def _():
        wait((W_HERE, 0), (W_HERE, 1))
        for d in WAYS:
            w_send((W_A_Y, 4 - d), w_half(0, 0, 0), 0, d)
        for d in WAYS:
            w_send((W_B_X, 4 - d), w_half(0, 0, 1), d, 0)
        for d in WAYS:
            w_send((W_A_X, 4 - d, 0), w_half(0, 0, 0), d, 0)
        for d in WAYS:
            w_send((W_B_Y, 0, 4 - d), w_half(0, 0, 1), 0, d)

    def add_w_forward(d):
        @task(WFA, d)
        def _():
            wait((W_A_Y, d))
            for dx in WAYS:
                w_send((W_A_X, 4 - dx, d), w_half(0, d, 0), dx, 0)

        @task(WFB, d)
        def _():
            wait((W_B_X, d))
            for dy in WAYS:
                w_send((W_B_Y, d, 4 - dy), w_half(d, 0, 1), 0, dy)

    for d in WAYS:
        add_w_forward(d)

    def w_names(dx):
        if dx == 0:
            names = [(W_A_Y, dy) for dy in WAYS]
        else:
            names = [(W_B_X, dx)] + [(W_A_X, dx, dy) for dy in range(4)]
        return names + [(W_B_Y, dx, dy) for dy in WAYS]

    def add_w_core(dx):
        @task(WC, dx)
        def _():
            wait(*w_names(dx))
            block = wb.at[:, lax.rem(head_at(dx) + 4, NH)]
            copy((W_CORE, dx), block, block, core)

    for dx in range(4):
        add_w_core(dx)

    @task(SPREAD)
    def _():
        for i in range(1, NH):
            copy(
                (TOKENS, i),
                rows(tok, PART * peers[i], PART, PART),
                ta.at[h],
                dev(y, z, peers[i]),
            )

    @task(WO)
    def _():
        for i in range(1, NH):
            copy(
                (W_OUT, i),
                w_out.at[span(64 * y, 64), span(FEAT * peers[i], FEAT)],
                wo.at[h, y],
                dev(y, z, peers[i]),
            )

    @task(LN)
    def _():
        wait(*((TOKENS, i) for i in range(1, NH)))
        tok_own.wait()
        mod_op.wait()
        total = jnp.zeros((PART, 1), F32)
        for j in range(NH):
            total += jnp.sum(ta[j].astype(F32), axis=-1, keepdims=True)
        center = total / WIDTH
        total = jnp.zeros((PART, 1), F32)
        for j in range(NH):
            total += jnp.sum((ta[j].astype(F32) - center) ** 2, axis=-1, keepdims=True)
        scale = lax.rsqrt(total / WIDTH + 1e-06)
        for j in range(NH):
            cols = slice(FEAT * j, FEAT * (j + 1))
            normed = (ta[j].astype(F32) - center) * scale
            xb[0, :, cols] = (
                normed * (1.0 + mod[1:2, cols].astype(F32)) + mod[0:1, cols].astype(F32)
            ).astype(BF16)
        for i in range(4):
            ring_copy(1, 0, i)
            ring_copy(1, 1, i)

    def ring_copy(k, way, i):
        step = min(2 * k - 1 + way, 15)
        before = 0 if k == 1 else 2 * k - 3 + way
        half = pl.ds(PART // 2 * (i // 2), PART // 2)
        cols = pl.ds(WIDTH // 2 * (i % 2), WIDTH // 2)
        copy(
            (BLOCK, way, k, i),
            xb.at[before, half, cols],
            xb.at[step, half, cols],
            at_z(1 - 2 * way),
        )

    def add_ring(k, way, i):
        @task(RING, k, way, i)
        def _():
            wait((BLOCK, way, k - 1, i))
            ring_copy(k, way, i)

    for k in range(2, 9):
        for way in range(2):
            for i in range(4):
                if k < 8 or (way == 0) == (i < 2):
                    add_ring(k, way, i)

    def slot_names(s):
        if s == 0:
            return []
        if s == 15:
            return [(BLOCK, 0, 8, 0), (BLOCK, 0, 8, 1), (BLOCK, 1, 8, 2), (BLOCK, 1, 8, 3)]
        way, k = 1 - s % 2, (s + 1) // 2
        return [(BLOCK, way, k, i) for i in range(4)]

    @task(WOY)
    def _():
        wait(*((W_OUT, i) for i in range(1, NH)))
        wo_own.wait()
        for dy in WAYS:
            copy((W_OUT_Y, dy), wo.at[:, y], wo.at[:, y], at(0, dy))

    def kv_slot(b, j, yl):
        n = PART * SPLIT[b]
        return pl.ds(pl.multiple_of(NZ * PART * FIRST[b] + n * (2 * j + yl), PART), n)

    def add_batch(b):
        first, n = PART * FIRST[b], PART * SPLIT[b]

        def norm(v, gain):
            mean_square = jnp.mean(v * v, axis=-1, keepdims=True)
            return (v * lax.rsqrt(mean_square + 1e-06) * gain[...]).astype(BF16)

        @task(PROJ, b)
        def _():
            for dx in range(4):
                wait(*w_names(dx), (W_CORE, dx))
            for s in range(FIRST[b], FIRST[b] + SPLIT[b]):
                wait(*slot_names(s))
            if b == 0:
                for op in gain_ops:
                    op.wait()
            x = xb[FIRST[b] : FIRST[b] + SPLIT[b]].reshape(n, WIDTH)
            w = wb[...].reshape(WIDTH, 3 * HDIM)
            qkv = jnp.dot(x, w, preferred_element_type=F32)
            here = kv_slot(b, h, ylo)
            kv[here, 0:HDIM] = norm(qkv[:, HDIM : 2 * HDIM], k_gain)
            kv[here, HDIM : 2 * HDIM] = qkv[:, 2 * HDIM :].astype(BF16)
            mine = kv.at[here]
            qs = norm(qkv[:, :HDIM], q_gain).reshape(SPLIT[b], 2, HALF, HDIM)
            for yy in range(2 if WAY_OF[b] == STRAIGHT else 1):
                for dx in (0,) + WAYS:
                    if dx or yy:
                        there = dev(other_y if yy else y, z, head_at(dx))
                        copy((KV_BLOCK, b, (4 - dx) % 4, yy), mine, mine, there)
            if WAY_OF[b] != STRAIGHT:
                copy((KV_BLOCK, b, 0, 1), mine, mine, dev(other_y, z, h))
            for i in range(2):
                qb[i, HALF * FIRST[b] : HALF * (FIRST[b] + SPLIT[b])] = qs[:, i].reshape(
                    n // 2, HDIM
                )

        def pair(dx):
            start = NZ * first + 2 * n * head_at(dx)
            return rows(kv, start, 2 * n, PART)

        if WAY_OF[b] == Y_FIRST:

            @task(KVF, b, 0)
            def _():
                wait((KV_BLOCK, b, 0, 1))
                block = kv.at[kv_slot(b, h, 1 - ylo)]
                for dx in WAYS:
                    copy((KV_BLOCK, b, 4 - dx, 1), block, block, at(dx, 0))
                copy((KV_CORE, b, 0), pair(0), pair(0), core)

        def add_forward(dx):
            @task(KVF, b, dx)
            def _():
                wait((KV_BLOCK, b, dx, 0))
                block = kv.at[kv_slot(b, head_at(dx), ylo)]
                copy((KV_BLOCK, b, dx, 1), block, block, dev(other_y, z, h))

        if WAY_OF[b] == X_FIRST:
            for dx in WAYS:
                add_forward(dx)

        def add_core(dx):
            @task(KVC, b, dx)
            def _():
                wait(*((KV_BLOCK, b, dx, yy) for yy in range(2) if dx or yy))
                copy((KV_CORE, b, dx), pair(dx), pair(dx), core)

        for dx in WAYS if WAY_OF[b] == Y_FIRST else range(4):
            add_core(dx)

    for b in range(LAST + 1):
        add_batch(b)

    def kv_names(b):
        names = [(KV_BLOCK, b, dx, yy) for dx in range(4) for yy in range(2) if dx or yy]
        return names + [(KV_CORE, b, dx) for dx in range(4)]

    def attend(batches, where, start, end):
        b, n = batches
        for i in range(n):
            wait(*kv_names(b + i))
        keys = pl.ds(NZ * PART * FIRST[b], NZ * PART * sum(SPLIT[b : b + n]))

        def get(ref):
            return ref[where].reshape(ROWS // 2, HDIM)

        def put(ref, value):
            ref[where] = value.reshape(ref[where].shape)

        s = lax.dot_general(
            get(qb),
            kv[keys, 0:HDIM],
            (((1,), (1,)), ((), ())),
            preferred_element_type=F32,
        )
        top = jnp.max(s, axis=1, keepdims=True) * EXP2_SCALE
        if start:
            now = jnp.broadcast_to(top, (ROWS // 2, HDIM))
        else:
            before = get(m_s)
            now = jnp.maximum(before, top)
            factor = jnp.exp2(before - now)
        p = jnp.exp2(s * EXP2_SCALE - now[:, 0:1])
        o = jnp.dot(p.astype(BF16), kv[keys, HDIM:], preferred_element_type=F32)
        t = jnp.broadcast_to(jnp.sum(p, axis=1, keepdims=True), (ROWS // 2, HDIM))
        if not start:
            t += get(l_s) * factor
            o += get(a_s) * factor
        if end:
            put(os, (o / t).astype(BF16))
        else:
            put(m_s, now)
            put(l_s, t)
            put(a_s, o)

    def add_attention(g, j, early):
        @task(EA if early else LA, g, j)
        def _():
            if early:
                slots = slice(ROWS // 4 * g, ROWS // 4 * (g + 1))
                attend(EARLY[j], (slice(None), slots), j == 0, False)
            else:
                attend(LATE[j], g, not EARLY and j == 0, j == len(LATE) - 1)

    for g in range(2):
        for j in range(len(EARLY)):
            add_attention(g, j, True)
        for j in range(len(LATE)):
            add_attention(g, j, False)

    head_cols = span(HDIM * my_head, HDIM)

    def add_return(g):
        half = pl.ds(HALF * g, HALF)

        @task(BACK, g)
        def _():
            for s in reversed(range(NZ)):
                here = os.at[g, pl.ds(HALF * s, HALF)]
                if s == 0:
                    ob[h, half, head_cols] = os[g, 0:HALF]
                    continue
                k = 8 if s == 15 else (-((s + 1) // 2) if s % 2 else s // 2)
                copy((ATTENDED, g, s), here, ob.at[h, half, head_cols], at_z(k))

        @task(O, g)
        def _():
            drain(W_OUT_Y, ATTENDED, HEADS, HEADS_CORE)
            wait(*((ATTENDED, g, s) for s in range(1, NZ)))
            block = ob.at[h, half]
            copy((HEADS_CORE, g, 0), block, block, core)
            for dx in WAYS:
                copy((HEADS, g, 4 - dx), block, block, at(dx, 0))

        def add_core(dx):
            @task(OC, g, dx)
            def _():
                wait((HEADS, g, dx))
                block = ob.at[head_at(dx), half]
                copy((HEADS_CORE, g, dx), block, block, core)

        for dx in WAYS:
            add_core(dx)

    for g in range(2):
        add_return(g)

    def add_out(g):
        @task(OUT, g)
        def _():
            wait(*((W_OUT_Y, dy) for dy in WAYS))
            wait(*((HEADS_CORE, g, dx) for dx in range(4)))
            half = slice(HALF * g, HALF * (g + 1))
            projected = jnp.dot(
                ob[:, half].reshape(TOK // 2, 2048),
                wo[...].reshape(2048, FEAT),
                preferred_element_type=F32,
            )
            gate = mod[2:3, span(FEAT * h, FEAT)].astype(F32)
            out[:, half] = (gate * projected).astype(BF16).reshape(NH, HALF, FEAT)
            if g == 0:
                drain(W_OUT_Y, HEADS, HEADS_CORE)

    for g in range(2):
        add_out(g)

    assert set(ORDER) == set(tasks) and len(ORDER) == len(tasks)
    for name in ORDER:
        tasks[name]()
    drain()


def body(tokens, modulation, w_qkv, query_gain, key_gain, w_out):
    branch = pl.pallas_call(
        kernel,
        out_shape=jax.ShapeDtypeStruct((NH, PART, FEAT), BF16),
        in_specs=[pl.BlockSpec(memory_space=pltpu.HBM)] * 6,
        out_specs=pl.BlockSpec(memory_space=pltpu.VMEM),
        scratch_shapes=[
            pltpu.VMEM((3, WIDTH), BF16),
            pltpu.VMEM((1, HDIM), F32),
            pltpu.VMEM((1, HDIM), F32),
            pltpu.VMEM((2, 48, 3 * HDIM), BF16),
            pltpu.VMEM((NH, PART, FEAT), BF16),
            pltpu.VMEM((NZ, PART, WIDTH), BF16),
            pltpu.VMEM((2, NH, 2, 2, 48, 3 * HDIM), BF16),
            pltpu.VMEM((2, ROWS // 2, HDIM), BF16),
            pltpu.VMEM((NZ * ROWS, 2 * HDIM), BF16),
            pltpu.VMEM((NH, 4, 64, FEAT), BF16),
            pltpu.VMEM((2, ROWS // 2, HDIM), BF16),
            pltpu.VMEM((NH, PART, 2048), BF16),
            pltpu.VMEM((2, ROWS // 2, HDIM), F32),
            pltpu.VMEM((2, ROWS // 2, HDIM), F32),
            pltpu.VMEM((2, ROWS // 2, HDIM), F32),
            pltpu.SemaphoreType.DMA((16,)),
            pltpu.SemaphoreType.DMA((N_SEMS,)),
            pltpu.SemaphoreType.DMA((N_SEMS,)),
        ],
        compiler_params=pltpu.CompilerParams(
            collective_id=0, has_side_effects=True, vmem_limit_bytes=60 << 20
        ),
        name="branch",
    )(
        tokens[0],
        modulation[0],
        w_qkv.transpose(1, 0, 2),
        query_gain.reshape(1, HDIM),
        key_gain.reshape(1, HDIM),
        w_out,
    )
    return branch.reshape(1, TOK, FEAT)


def solution(mesh):
    in_specs = (
        P("grp", "ctx", "head"),
        P("grp", None, None),
        P(("ctx", "grp"), None, "head"),
        P(),
        P(),
        P("head", None),
    )
    out_specs = P("grp", "ctx", "head")
    return jax.shard_map(body, mesh=mesh, in_specs=in_specs, out_specs=out_specs, check_vma=False)
```

```python
import functools

import jax
import jax.numpy as jnp
import numpy as np
from jax import lax
from jax.experimental import pallas as pl
from jax.experimental.pallas import tpu as pltpu
from jax.sharding import PartitionSpec as P

MESH = pl.DeviceIdType.MESH
BF16 = jnp.bfloat16
F32 = jnp.float32
NZ, NH, HDIM = 16, 8, 128
TOK, FEAT, WIDTH = 256, 384, 3072
PART = 32
SPLIT = (4, 4, 4, 3, 1)
FIRST = tuple(sum(SPLIT[:b]) for b in range(len(SPLIT)))
LAST = len(SPLIT) - 1
Y_FIRST, X_FIRST, STRAIGHT = range(3)
WAY_OF = (X_FIRST, Y_FIRST, STRAIGHT, STRAIGHT, STRAIGHT)
ROWS = NZ * PART
HALF = PART // 2
EARLY = ((0, 1), (1, 1), (2, 1))
LATE = ((3, 2),)
N_SEMS = 240
WAYS = (1, 3, 2)
(
    W_SENT, W_HERE, TOKENS, W_OUT, BLOCK, W_A_Y, W_B_X, W_A_X, W_B_Y, W_CORE,
    KV_BLOCK, KV_CORE, W_OUT_Y, ATTENDED, HEADS, HEADS_CORE,
) = range(16)
(
    W1, SPREAD, WO, LN, RING, WD, WFA, WFB, WC, PROJ, KVF, KVC, WOY, EA, LA, BACK, O, OC, OUT,
) = range(19)
EXP2_SCALE = float(HDIM ** (-0.5) * np.log2(np.e))
ORDER = (
    (W1,), (SPREAD,), (WO,), (LN,), (RING, 2, 0, 0), (RING, 2, 1, 0), (WD,), (RING, 2, 0, 1),
    (RING, 2, 1, 1), (RING, 2, 0, 2), (RING, 2, 1, 2), (RING, 2, 0, 3), (RING, 2, 1, 3),
    (WFA, 1), (WFB, 1), (WFA, 3), (WFB, 3), (RING, 3, 0, 0), (RING, 3, 1, 0), (RING, 3, 0, 1),
    (RING, 3, 1, 1), (WFA, 2), (WFB, 2), (RING, 3, 0, 2), (RING, 3, 1, 2), (WC, 0),
    (RING, 3, 0, 3), (RING, 3, 1, 3), (RING, 4, 0, 0), (RING, 4, 1, 0), (RING, 4, 0, 1),
    (RING, 4, 1, 1), (RING, 4, 0, 2), (RING, 4, 1, 2), (WC, 1), (WC, 3), (RING, 4, 0, 3),
    (RING, 4, 1, 3), (WC, 2), (RING, 5, 0, 0), (RING, 5, 1, 0), (RING, 5, 0, 1),
    (RING, 5, 1, 1), (PROJ, 0), (RING, 5, 0, 2), (RING, 5, 1, 2), (RING, 5, 0, 3),
    (RING, 5, 1, 3), (PROJ, 1), (RING, 6, 0, 0), (RING, 6, 1, 0), (RING, 6, 0, 1),
    (RING, 6, 1, 1), (KVF, 0, 1), (KVF, 0, 3), (KVC, 0, 0), (RING, 6, 0, 2), (RING, 6, 1, 2),
    (RING, 6, 0, 3), (KVF, 1, 0), (RING, 6, 1, 3), (RING, 7, 0, 0), (RING, 7, 1, 0),
    (KVF, 0, 2), (KVC, 0, 1), (RING, 7, 0, 1), (RING, 7, 1, 1), (RING, 7, 0, 2),
    (RING, 7, 1, 2), (PROJ, 2), (KVC, 0, 3), (RING, 8, 0, 0), (KVC, 1, 3), (RING, 7, 1, 3),
    (KVC, 0, 2), (KVC, 1, 1), (RING, 7, 0, 3), (KVC, 1, 2), (RING, 8, 0, 1), (RING, 8, 1, 2),
    (EA, 0, 0), (RING, 8, 1, 3), (PROJ, 3), (KVC, 2, 0), (EA, 0, 1), (KVC, 2, 1), (PROJ, 4),
    (KVC, 2, 3), (KVC, 2, 2), (KVC, 3, 0), (EA, 1, 0), (WOY,), (EA, 0, 2), (KVC, 4, 0),
    (KVC, 3, 1), (KVC, 3, 3), (EA, 1, 1), (KVC, 3, 2), (KVC, 4, 1), (KVC, 4, 3), (KVC, 4, 2),
    (EA, 1, 2), (LA, 0, 0), (BACK, 0), (LA, 1, 0), (BACK, 1), (O, 0), (O, 1), (OC, 0, 1),
    (OC, 0, 3), (OC, 0, 2), (OC, 1, 1), (OC, 1, 3), (OUT, 0), (OC, 1, 2), (OUT, 1),
)


def head_of(z):
    return lax.rem(z, 4) * 4 + z // 4


def kernel(
    tok,
    mod_hbm,
    w_in,
    q_gain_hbm,
    k_gain_hbm,
    w_out,
    out,
    mod,
    q_gain,
    k_gain,
    wp,
    ta,
    xb,
    wb,
    qb,
    kv,
    wo,
    os,
    ob,
    m_s,
    l_s,
    a_s,
    local_sem,
    send_sem,
    recv_sem,
):
    c = lax.axis_index("ctx")
    h = lax.axis_index("head")
    yhi = lax.axis_index("grp")
    ylo, z = c // NZ, lax.rem(c, NZ)
    y = 2 * yhi + ylo

    def dev(y, z, h):
        return (lax.rem(y, 2) * NZ + z, h, y // 2)

    def at_z(k):
        return dev(y, lax.rem(z + k + NZ, NZ), h)

    def at_y(k):
        return dev(lax.rem(y + k + 4, 4), z, h)

    def head_at(k):
        return lax.rem(h + 2 * k + NH, NH)

    def at(dx, dy):
        return dev(lax.rem(y + dy, 4), z, head_at(dx))

    other_y = y + 1 - 2 * ylo
    core = dev(y, z, h + 1 - 2 * lax.rem(h, 2))
    bits = (lax.rem(h, 2), lax.rem(h // 2, 2), h // 4)
    peers = []
    for i in range(NH):
        flips = (i & 1, (i >> 1) & 1, i >> 2)
        peers.append(
            sum((b + f - 2 * b * f) * w for b, f, w in zip(bits, flips, (1, 2, 4)))
        )

    count = [0]
    started = []
    ops = {}

    def copy(name, src, dst, device, recv=None, start=True):
        i = count[0]
        count[0] += 1
        assert i < N_SEMS
        op = pltpu.make_async_remote_copy(
            src_ref=src,
            dst_ref=dst,
            send_sem=send_sem.at[i],
            recv_sem=recv_sem.at[i if recv is None else recv],
            device_id=device,
            device_id_type=MESH,
        )
        if start:
            op.start()
            started.append((name, op))
        assert name not in ops
        ops[name] = op

    def drain(*later):
        for name, op in started:
            if name[0] not in later:
                op.wait_send()
        started[:] = [sent for sent in started if sent[0][0] in later]

    waited = set()

    def wait(*names):
        for name in names:
            if name not in waited:
                waited.add(name)
                ops[name].wait_recv()

    def rows(ref, start, size, unit):
        return ref.at[pl.ds(pl.multiple_of(start, unit), size)]

    def span(start, size):
        return pl.ds(pl.multiple_of(start, size), size)

    my_head = head_of(z)
    piece = lax.rem(h + 4, NH)
    w_targets = [
        dev(y, head_of(2 * h + p), lax.rem(z // 2 + 4, NH)) for p in range(2)
    ]

    locals_ = []

    def local(src, dst):
        op = pltpu.make_async_copy(src, dst, local_sem.at[len(locals_)])
        op.start()
        locals_.append(op)
        return op

    wp_ops = [
        local(
            w_in.at[j, :, pl.ds(p * HDIM, HDIM)],
            wp.at[p, :, pl.ds(j * HDIM, HDIM)],
        )
        for p in range(2)
        for j in range(3)
    ]
    tok_own = local(rows(tok, PART * h, PART, PART), ta.at[h])
    mod_op = local(mod_hbm, mod)
    gain_ops = [local(q_gain_hbm, q_gain), local(k_gain_hbm, k_gain)]
    wo_own = local(w_out.at[span(64 * y, 64), span(FEAT * h, FEAT)], wo.at[h, y])

    barrier = pltpu.get_barrier_semaphore()
    greet = [dev(y, z, peers[i]) for i in range(1, NH)]
    greet += [at_z(k) for k in range(1, NZ)]
    greet += [at(dx, dy) for dx in range(4) for dy in WAYS]
    greet += [dev(y, 2 * piece + s, my_head // 2) for s in range(2)]
    for d in greet:
        pl.semaphore_signal(barrier, inc=1, device_id=d, device_id_type=MESH)
    pl.semaphore_wait(barrier, len(greet))

    tasks = {}

    def task(*name):
        def add(f):
            tasks[name] = f
            return f

        return add

    @task(W1)
    def _():
        for op in wp_ops:
            op.wait()
        base = count[0]
        for p in range(2):
            copy(
                (W_SENT, p),
                wp.at[p],
                wb.at[ylo, z // 2, lax.rem(z, 2), yhi],
                w_targets[p],
                recv=base + lax.rem(z, 2),
            )
        for s in range(2):
            copy(
                (W_HERE, s),
                wp.at[s],
                wb.at[ylo, piece, s, yhi],
                core,
                recv=base + s,
                start=False,
            )

    def w_half(dx, dy, s):
        yy = lax.rem(y + dy, 4)
        return wb.at[lax.rem(yy, 2), lax.rem(head_at(dx) + 4, NH), s, yy // 2]

    def w_send(name, block, dx, dy):
        copy(name, block, block, at(dx, dy))

    @task(WD)
    def _():
        wait((W_HERE, 0), (W_HERE, 1))
        for d in WAYS:
            w_send((W_A_Y, 4 - d), w_half(0, 0, 0), 0, d)
        for d in WAYS:
            w_send((W_B_X, 4 - d), w_half(0, 0, 1), d, 0)
        for d in WAYS:
            w_send((W_A_X, 4 - d, 0), w_half(0, 0, 0), d, 0)
        for d in WAYS:
            w_send((W_B_Y, 0, 4 - d), w_half(0, 0, 1), 0, d)

    def add_w_forward(d):
        @task(WFA, d)
        def _():
            wait((W_A_Y, d))
            for dx in WAYS:
                w_send((W_A_X, 4 - dx, d), w_half(0, d, 0), dx, 0)

        @task(WFB, d)
        def _():
            wait((W_B_X, d))
            for dy in WAYS:
                w_send((W_B_Y, d, 4 - dy), w_half(d, 0, 1), 0, dy)

    for d in WAYS:
        add_w_forward(d)

    def w_names(dx):
        if dx == 0:
            names = [(W_A_Y, dy) for dy in WAYS]
        else:
            names = [(W_B_X, dx)] + [(W_A_X, dx, dy) for dy in range(4)]
        return names + [(W_B_Y, dx, dy) for dy in WAYS]

    def add_w_core(dx):
        @task(WC, dx)
        def _():
            wait(*w_names(dx))
            block = wb.at[:, lax.rem(head_at(dx) + 4, NH)]
            copy((W_CORE, dx), block, block, core)

    for dx in range(4):
        add_w_core(dx)

    @task(SPREAD)
    def _():
        for i in range(1, NH):
            copy(
                (TOKENS, i),
                rows(tok, PART * peers[i], PART, PART),
                ta.at[h],
                dev(y, z, peers[i]),
            )

    @task(WO)
    def _():
        for i in range(1, NH):
            copy(
                (W_OUT, i),
                w_out.at[span(64 * y, 64), span(FEAT * peers[i], FEAT)],
                wo.at[h, y],
                dev(y, z, peers[i]),
            )

    @task(LN)
    def _():
        wait(*((TOKENS, i) for i in range(1, NH)))
        tok_own.wait()
        mod_op.wait()
        total = jnp.zeros((PART, 1), F32)
        for j in range(NH):
            total += jnp.sum(ta[j].astype(F32), axis=-1, keepdims=True)
        center = total / WIDTH
        total = jnp.zeros((PART, 1), F32)
        for j in range(NH):
            total += jnp.sum((ta[j].astype(F32) - center) ** 2, axis=-1, keepdims=True)
        scale = lax.rsqrt(total / WIDTH + 1e-06)
        for j in range(NH):
            cols = slice(FEAT * j, FEAT * (j + 1))
            normed = (ta[j].astype(F32) - center) * scale
            xb[0, :, cols] = (
                normed * (1.0 + mod[1:2, cols].astype(F32)) + mod[0:1, cols].astype(F32)
            ).astype(BF16)
        for i in range(4):
            ring_copy(1, 0, i)
            ring_copy(1, 1, i)

    def ring_copy(k, way, i):
        step = min(2 * k - 1 + way, 15)
        before = 0 if k == 1 else 2 * k - 3 + way
        half = pl.ds(PART // 2 * (i // 2), PART // 2)
        cols = pl.ds(WIDTH // 2 * (i % 2), WIDTH // 2)
        copy(
            (BLOCK, way, k, i),
            xb.at[before, half, cols],
            xb.at[step, half, cols],
            at_z(1 - 2 * way),
        )

    def add_ring(k, way, i):
        @task(RING, k, way, i)
        def _():
            wait((BLOCK, way, k - 1, i))
            ring_copy(k, way, i)

    for k in range(2, 9):
        for way in range(2):
            for i in range(4):
                if k < 8 or (way == 0) == (i < 2):
                    add_ring(k, way, i)

    def slot_names(s):
        if s == 0:
            return []
        if s == 15:
            return [(BLOCK, 0, 8, 0), (BLOCK, 0, 8, 1), (BLOCK, 1, 8, 2), (BLOCK, 1, 8, 3)]
        way, k = 1 - s % 2, (s + 1) // 2
        return [(BLOCK, way, k, i) for i in range(4)]

    @task(WOY)
    def _():
        wait(*((W_OUT, i) for i in range(1, NH)))
        wo_own.wait()
        for dy in WAYS:
            copy((W_OUT_Y, dy), wo.at[:, y], wo.at[:, y], at(0, dy))

    def kv_slot(b, j, yl):
        n = PART * SPLIT[b]
        return pl.ds(pl.multiple_of(NZ * PART * FIRST[b] + n * (2 * j + yl), PART), n)

    def add_batch(b):
        first, n = PART * FIRST[b], PART * SPLIT[b]

        def norm(v, gain):
            mean_square = jnp.mean(v * v, axis=-1, keepdims=True)
            return (v * lax.rsqrt(mean_square + 1e-06) * gain[...]).astype(BF16)

        @task(PROJ, b)
        def _():
            for dx in range(4):
                wait(*w_names(dx), (W_CORE, dx))
            for s in range(FIRST[b], FIRST[b] + SPLIT[b]):
                wait(*slot_names(s))
            if b == 0:
                for op in gain_ops:
                    op.wait()
            x = xb[FIRST[b] : FIRST[b] + SPLIT[b]].reshape(n, WIDTH)
            w = wb[...].reshape(WIDTH, 3 * HDIM)
            qkv = jnp.dot(x, w, preferred_element_type=F32)
            here = kv_slot(b, h, ylo)
            kv[here, 0:HDIM] = norm(qkv[:, HDIM : 2 * HDIM], k_gain)
            kv[here, HDIM : 2 * HDIM] = qkv[:, 2 * HDIM :].astype(BF16)
            mine = kv.at[here]
            qs = norm(qkv[:, :HDIM], q_gain).reshape(SPLIT[b], 2, HALF, HDIM)
            for yy in range(2 if WAY_OF[b] == STRAIGHT else 1):
                for dx in (0,) + WAYS:
                    if dx or yy:
                        there = dev(other_y if yy else y, z, head_at(dx))
                        copy((KV_BLOCK, b, (4 - dx) % 4, yy), mine, mine, there)
            if WAY_OF[b] != STRAIGHT:
                copy((KV_BLOCK, b, 0, 1), mine, mine, dev(other_y, z, h))
            for i in range(2):
                qb[i, HALF * FIRST[b] : HALF * (FIRST[b] + SPLIT[b])] = qs[:, i].reshape(
                    n // 2, HDIM
                )

        def pair(dx):
            start = NZ * first + 2 * n * head_at(dx)
            return rows(kv, start, 2 * n, PART)

        if WAY_OF[b] == Y_FIRST:

            @task(KVF, b, 0)
            def _():
                wait((KV_BLOCK, b, 0, 1))
                block = kv.at[kv_slot(b, h, 1 - ylo)]
                for dx in WAYS:
                    copy((KV_BLOCK, b, 4 - dx, 1), block, block, at(dx, 0))
                copy((KV_CORE, b, 0), pair(0), pair(0), core)

        def add_forward(dx):
            @task(KVF, b, dx)
            def _():
                wait((KV_BLOCK, b, dx, 0))
                block = kv.at[kv_slot(b, head_at(dx), ylo)]
                copy((KV_BLOCK, b, dx, 1), block, block, dev(other_y, z, h))

        if WAY_OF[b] == X_FIRST:
            for dx in WAYS:
                add_forward(dx)

        def add_core(dx):
            @task(KVC, b, dx)
            def _():
                wait(*((KV_BLOCK, b, dx, yy) for yy in range(2) if dx or yy))
                copy((KV_CORE, b, dx), pair(dx), pair(dx), core)

        for dx in WAYS if WAY_OF[b] == Y_FIRST else range(4):
            add_core(dx)

    for b in range(LAST + 1):
        add_batch(b)

    def kv_names(b):
        names = [(KV_BLOCK, b, dx, yy) for dx in range(4) for yy in range(2) if dx or yy]
        return names + [(KV_CORE, b, dx) for dx in range(4)]

    def attend(batches, where, start, end):
        b, n = batches
        for i in range(n):
            wait(*kv_names(b + i))
        keys = pl.ds(NZ * PART * FIRST[b], NZ * PART * sum(SPLIT[b : b + n]))

        def get(ref):
            return ref[where].reshape(ROWS // 2, HDIM)

        def put(ref, value):
            ref[where] = value.reshape(ref[where].shape)

        s = lax.dot_general(
            get(qb),
            kv[keys, 0:HDIM],
            (((1,), (1,)), ((), ())),
            preferred_element_type=F32,
        )
        top = jnp.max(s, axis=1, keepdims=True) * EXP2_SCALE
        if start:
            now = jnp.broadcast_to(top, (ROWS // 2, HDIM))
        else:
            before = get(m_s)
            now = jnp.maximum(before, top)
            factor = jnp.exp2(before - now)
        p = jnp.exp2(s * EXP2_SCALE - now[:, 0:1])
        o = jnp.dot(p.astype(BF16), kv[keys, HDIM:], preferred_element_type=F32)
        t = jnp.broadcast_to(jnp.sum(p, axis=1, keepdims=True), (ROWS // 2, HDIM))
        if not start:
            t += get(l_s) * factor
            o += get(a_s) * factor
        if end:
            put(os, (o / t).astype(BF16))
        else:
            put(m_s, now)
            put(l_s, t)
            put(a_s, o)

    def add_attention(g, j, early):
        @task(EA if early else LA, g, j)
        def _():
            if early:
                slots = slice(ROWS // 4 * g, ROWS // 4 * (g + 1))
                attend(EARLY[j], (slice(None), slots), j == 0, False)
            else:
                attend(LATE[j], g, not EARLY and j == 0, j == len(LATE) - 1)

    for g in range(2):
        for j in range(len(EARLY)):
            add_attention(g, j, True)
        for j in range(len(LATE)):
            add_attention(g, j, False)

    head_cols = span(HDIM * my_head, HDIM)

    def add_return(g):
        half = pl.ds(HALF * g, HALF)

        @task(BACK, g)
        def _():
            for s in reversed(range(NZ)):
                here = os.at[g, pl.ds(HALF * s, HALF)]
                if s == 0:
                    ob[h, half, head_cols] = os[g, 0:HALF]
                    continue
                k = 8 if s == 15 else (-((s + 1) // 2) if s % 2 else s // 2)
                copy((ATTENDED, g, s), here, ob.at[h, half, head_cols], at_z(k))

        @task(O, g)
        def _():
            drain(W_OUT_Y, ATTENDED, HEADS, HEADS_CORE)
            wait(*((ATTENDED, g, s) for s in range(1, NZ)))
            block = ob.at[h, half]
            copy((HEADS_CORE, g, 0), block, block, core)
            for dx in WAYS:
                copy((HEADS, g, 4 - dx), block, block, at(dx, 0))

        def add_core(dx):
            @task(OC, g, dx)
            def _():
                wait((HEADS, g, dx))
                block = ob.at[head_at(dx), half]
                copy((HEADS_CORE, g, dx), block, block, core)

        for dx in WAYS:
            add_core(dx)

    for g in range(2):
        add_return(g)

    def add_out(g):
        @task(OUT, g)
        def _():
            wait(*((W_OUT_Y, dy) for dy in WAYS))
            wait(*((HEADS_CORE, g, dx) for dx in range(4)))
            half = slice(HALF * g, HALF * (g + 1))
            projected = jnp.dot(
                ob[:, half].reshape(TOK // 2, 2048),
                wo[...].reshape(2048, FEAT),
                preferred_element_type=F32,
            )
            gate = mod[2:3, span(FEAT * h, FEAT)].astype(F32)
            out[:, half] = (gate * projected).astype(BF16).reshape(NH, HALF, FEAT)
            if g == 0:
                drain(W_OUT_Y, HEADS, HEADS_CORE)

    for g in range(2):
        add_out(g)

    assert set(ORDER) == set(tasks) and len(ORDER) == len(tasks)
    for name in ORDER:
        tasks[name]()
    drain()


def body(tokens, modulation, w_qkv, query_gain, key_gain, w_out):
    branch = pl.pallas_call(
        kernel,
        out_shape=jax.ShapeDtypeStruct((NH, PART, FEAT), BF16),
        in_specs=[pl.BlockSpec(memory_space=pltpu.HBM)] * 6,
        out_specs=pl.BlockSpec(memory_space=pltpu.VMEM),
        scratch_shapes=[
            pltpu.VMEM((3, WIDTH), BF16),
            pltpu.VMEM((1, HDIM), F32),
            pltpu.VMEM((1, HDIM), F32),
            pltpu.VMEM((2, 48, 3 * HDIM), BF16),
            pltpu.VMEM((NH, PART, FEAT), BF16),
            pltpu.VMEM((NZ, PART, WIDTH), BF16),
            pltpu.VMEM((2, NH, 2, 2, 48, 3 * HDIM), BF16),
            pltpu.VMEM((2, ROWS // 2, HDIM), BF16),
            pltpu.VMEM((NZ * ROWS, 2 * HDIM), BF16),
            pltpu.VMEM((NH, 4, 64, FEAT), BF16),
            pltpu.VMEM((2, ROWS // 2, HDIM), BF16),
            pltpu.VMEM((NH, PART, 2048), BF16),
            pltpu.VMEM((2, ROWS // 2, HDIM), F32),
            pltpu.VMEM((2, ROWS // 2, HDIM), F32),
            pltpu.VMEM((2, ROWS // 2, HDIM), F32),
            pltpu.SemaphoreType.DMA((16,)),
            pltpu.SemaphoreType.DMA((N_SEMS,)),
            pltpu.SemaphoreType.DMA((N_SEMS,)),
        ],
        compiler_params=pltpu.CompilerParams(
            collective_id=0, has_side_effects=True, vmem_limit_bytes=60 << 20
        ),
        name="branch",
    )(
        tokens[0],
        modulation[0],
        w_qkv.transpose(1, 0, 2),
        query_gain.reshape(1, HDIM),
        key_gain.reshape(1, HDIM),
        w_out,
    )
    return branch.reshape(1, TOK, FEAT)


def solution(mesh):
    in_specs = (
        P("grp", "ctx", "head"),
        P("grp", None, None),
        P(("ctx", "grp"), None, "head"),
        P(),
        P(),
        P("head", None),
    )
    out_specs = P("grp", "ctx", "head")
    return jax.shard_map(body, mesh=mesh, in_specs=in_specs, out_specs=out_specs, check_vma=False)
```
